32 devices in a mesh: groups: 2 (over y), ctx: 4 (over x, core), tp: 4 (over z).
Axes of the slice: x: 2, y: 2, z: 4, core: 2. Of those that a mesh axis runs over, the one named last changes fastest.
Arguments:
- question_hidden: bfloat16 [256, 8192], P(('groups', 'ctx')), parts along dimension 0, may hold values from -1800 to 1800
- recomp_hidden: bfloat16 [512, 8192], P(('groups', 'ctx')), parts along dimension 0, may hold values from -1800 to 1800
- norm_gain: bfloat16 [8192], replicated, may hold values from 0.099609375 to 1.8984375
- w_query: bfloat16 [8192, 8192], P('ctx', 'tp'), may hold values from -0.0625 to 0.0625
- w_keyval: bfloat16 [8192, 2, 1024], P('ctx', None, 'tp'), may hold values from -0.25 to 0.25
- pool_codes: bfloat16 [384, 2, 64, 1024], P(('groups', 'ctx'), None, None, 'tp'), parts along dimension 0, may hold values from -127 to 127
- pool_scales: bfloat16 [384, 2, 8], P(('groups', 'ctx'), None, 'tp'), parts along dimension 0, may hold values from 0.025 to 2
- block_owner: int32 [256, 1], P('groups'), parts along dimension 0, may hold values from 0 to 3; in each aligned block of 32 rows (0 to 31, 32 to 63, ...) at most 16 rows name the same one
- block_slot: int32 [256], P('groups'), parts along dimension 0, may hold values from 0 to 47
- recomp_pos: int32 [512], P('groups'), parts along dimension 0, may hold values from 0 to 8191, as said below
Outputs:
- attended: bfloat16 [256, 8192], P(('groups', 'ctx'), 'tp'), parts along dimension 0
- kv_cache: bfloat16 [2, 16384, 1024], P(None, ('groups', 'ctx'), 'tp'), parts along dimension 1
The draws below stay inside these ranges and needn't reach their ends.
There are 2 independent parts, one for each index of `groups`. The reference program is written for one: setup_inputs(seed, part) draws one part's arguments, and reference() takes and returns one part's arrays. A program takes and returns all parts, laid end to end along the dimension named above; an argument that names none is the same for every part. Nothing has to cross between parts.
Inputs may be any that keep to these rules, and one draw needn't show every extreme that they name: Among the 32 context blocks of each index of ctx (rows of block_owner in aligned blocks), at most 16 name the same pool shard. `recomp_pos`: 256 distinct positions in no particular order; the first and the last context position are always listed.
All inputs are finite; a program needn't handle non-finite values.
Results may differ from the reference program's by a relative error of at most 0.018.
The reference program's roundings to bfloat16 on the way (of `normed_question`, `normed_recomp`, `query`, `question_kv`, `recomp_kv`, `cached` and `weights_low`) count: a program that leaves them out, or rounds other values in their place, can miss the bound.
Values may be sent and summed in bfloat16 or wider, within the bound.
A program may use at most 128 MiB of HBM per device.

```python
import math
import jax
import jax.numpy as jnp
import numpy as np
from jax import lax

D = 8192
NH = 64
KVH = 8
HD = 128
GROUP = 8
BLOCK = 64
POOL_DEV = 48
QTOK = 128
RECOMP = 256
CTX_TOK = 8192
BLK_DEV = 32
CTX_BLOCKS = 128
POOL_BLOCKS = 192
OWNERS = 4
MOST = 16


def hidden_rows(key, row_count, salt):
    key_cols = jax.random.fold_in(key, 7)
    key_base = jax.random.fold_in(key, salt)
    key_rows = jax.random.fold_in(key, salt + 100)
    column_scale = jnp.exp(jax.random.uniform(key_cols, (D,), jnp.float32, 0.0, math.log(10.0)))
    row_scale = jnp.exp(jax.random.uniform(key_rows, (row_count, 1), jnp.float32, 0.0, math.log(10.0)))
    base_draw = jnp.clip(jax.random.normal(key_base, (row_count, D), jnp.float32), -4.0, 4.0)
    return (base_draw * column_scale[None, :] * row_scale).astype(jnp.bfloat16)


def draw_question_hidden(key, part):
    return hidden_rows(key, QTOK, 1)


def draw_recomp_hidden(key, part):
    return hidden_rows(key, RECOMP, 2)


def draw_pool_codes(key, part):
    shape_all = (POOL_BLOCKS, 2, BLOCK, KVH * HD)
    values = jax.random.uniform(key, shape_all, jnp.float32, -127.0, 127.0)
    return values.astype(jnp.bfloat16)


def draw_pool_scales(key, part):
    key_base = jax.random.fold_in(key, 1)
    base_scale = jnp.exp(jax.random.uniform(key_base, (POOL_BLOCKS, 2, KVH), jnp.float32, math.log(0.025), math.log(0.05)))
    return base_scale.astype(jnp.bfloat16)


def draw_recomp_pos(key, part):
    key_pick = jax.random.fold_in(key, 11)
    key_order = jax.random.fold_in(key, 12)
    shuffled = jax.random.permutation(key_pick, CTX_TOK - 2)[:RECOMP - 2] + 1
    inner_pos = shuffled.astype(jnp.int32)
    listed = jnp.concatenate([jnp.zeros((1,), jnp.int32), inner_pos, jnp.full((1,), CTX_TOK - 1, jnp.int32)])
    return jax.random.permutation(key_order, listed).astype(jnp.int32)


def plant(array, key, least, top_value):
    longest = array.shape.index(max(array.shape))
    spots = []
    for shift in (0, 1):
        where = [jax.random.randint(jax.random.fold_in(key, axis), (), 0, length) for axis, length in enumerate(array.shape)]
        where[longest] = (where[longest] + shift) % array.shape[longest]
        spots.append(tuple(where))
    return array.at[spots[0]].set(least).at[spots[1]].set(top_value)


def shard_levels(stream_key, extent, shards, least, largest):
    factor_of, own = 1.0, jax.random.fold_in(stream_key, 6)
    for axis_at, parts in shards:
        steps = jnp.exp(jax.random.uniform(jax.random.fold_in(own, axis_at), (parts,), jnp.float32, least / len(shards), largest / len(shards)))
        factor_of = factor_of * jnp.repeat(steps, extent[axis_at] // parts).reshape([-1 if axis == axis_at else 1 for axis in range(len(extent))])
    return factor_of


def routed_block(key, own, number, rows, amount, top, bound, lean):
    sequence = jax.random.permutation(key, amount)
    crowded, usual = portions_of(amount, rows * top, bound, lean, True), portions_of(amount, rows * top, bound, lean, False)
    places = jnp.arange(amount)

    def named(tallies, offset_by):
        used = int((tallies > 0).sum())
        fixed = max(1, used // 4)
        shifted = fixed + (places - fixed + offset_by * (used - fixed)) % max(1, amount - fixed)
        return jnp.zeros((amount,), jnp.int32).at[sequence[jnp.where(places < fixed, places, shifted)]].set(jnp.asarray(tallies, jnp.int32))

    tallies = jnp.where(number % 4 == 0, named(crowded, number // 4), named(usual, number - number // 4 - 1))
    mixed = jax.random.permutation(jax.random.fold_in(own, 3), amount)
    source_of, sink = mixed[0:amount // 2 * 2:2], mixed[1:amount // 2 * 2:2]
    slack = jnp.minimum(tallies[source_of] - 1, bound - tallies[sink]) // 2
    slack = jnp.where((source_of == sequence[0]) | (sink == sequence[0]) | (tallies[sink] == 0), 0, jnp.maximum(slack, 0))
    shifted = jax.random.randint(jax.random.fold_in(own, 4), (amount // 2,), 0, 1 << 20) % (slack + 1)
    tallies = tallies.at[source_of].add(-shifted).at[sink].add(shifted)
    members = jnp.searchsorted(jnp.cumsum(tallies), jnp.arange(rows * top), side="right").astype(jnp.int32)
    grid = members.reshape(top, rows).T
    grid = grid[jax.random.permutation(jax.random.fold_in(own, 1), rows)]
    offset_by = jax.random.randint(jax.random.fold_in(own, 2), (rows, 1), 0, top)
    return jnp.take_along_axis(grid, (jnp.arange(top)[None, :] + offset_by) % top, axis=1)


def portions_of(count, total, bound, lean, full):
    loads = [(1 << 20) // math.isqrt(grade ** lean) + 1 for grade in range(1, count + 1)]
    largest = bound if full else min(bound, max(-(-total // count), total * loads[0] // sum(loads)))
    least = 1 if total - largest >= count - 1 else 0
    counts, spare = [largest] + [least] * (count - 1), total - largest - least * (count - 1)
    while spare > 0:
        free = [i for i in range(1, count) if counts[i] < largest] or [i for i in range(1, count) if counts[i] < bound]
        pool, left = sum([loads[i] for i in free]), spare
        for i in free:
            addition = min(bound - counts[i], max(1, left * loads[i] // pool), spare)
            counts[i] = counts[i] + addition
            spare = spare - addition
    return np.array(counts)


def normal_values(key, shape, width, limit, split=(), held_as=jnp.bfloat16):
    array = width * jax.random.normal(key, shape, jnp.float32)
    if split:
        array = array * shard_levels(key, shape, split, -0.22, 0.18)
    return jnp.clip(array, -limit, limit).astype(held_as)


def setup_inputs(seed: int = 0, part: int = 0) -> dict:
    key_of = jax.random.split(jax.random.key(seed), 11)
    own_keys = jax.random.split(jax.random.fold_in(key_of[10], part), 11)
    question_hidden = draw_question_hidden(jax.random.fold_in(jax.random.fold_in(key_of[10], part), 71), part)
    recomp_hidden = draw_recomp_hidden(jax.random.fold_in(jax.random.fold_in(key_of[10], part), 71), part)
    norm_gain = jnp.clip(1.0 + 0.18 * jax.random.normal(key_of[2], (D,), jnp.float32), 0.099609375, 1.8984375).astype(jnp.bfloat16)
    w_query = normal_values(key_of[3], (D, NH * HD), D ** -0.5, 0.0625, ((0, 4), (1, 4)))
    w_keyval = normal_values(key_of[4], (D, 2, KVH * HD), (D // 16) ** -0.5, 0.25, ((0, 4), (2, 4)))
    pool_codes = draw_pool_codes(jax.random.fold_in(jax.random.fold_in(key_of[10], part), 71), part)
    pool_scales = draw_pool_scales(jax.random.fold_in(jax.random.fold_in(key_of[10], part), 71), part)
    block_owner_keys = jax.random.split(jax.random.fold_in(own_keys[7], 1), CTX_BLOCKS // BLK_DEV)
    block_owner_turns = jax.random.permutation(jax.random.fold_in(own_keys[7], 3), CTX_BLOCKS // BLK_DEV)
    block_owner = jax.vmap(lambda own, number: routed_block(jax.random.fold_in(own_keys[7], 2), own, number, BLK_DEV, OWNERS, 1, MOST, 2))(block_owner_keys, block_owner_turns).reshape((CTX_BLOCKS, 1))
    block_slot = plant(jax.random.randint(own_keys[8], (CTX_BLOCKS,), 0, POOL_DEV), jax.random.fold_in(own_keys[8], 1), 0, POOL_DEV - 1).astype(jnp.int32)
    recomp_pos = draw_recomp_pos(jax.random.fold_in(jax.random.fold_in(key_of[10], part), 71), part)
    return dict(question_hidden=question_hidden, recomp_hidden=recomp_hidden, norm_gain=norm_gain, w_query=w_query, w_keyval=w_keyval, pool_codes=pool_codes, pool_scales=pool_scales, block_owner=block_owner, block_slot=block_slot, recomp_pos=recomp_pos)


norm_eps = 1e-05

def rms_rows(hidden, norm_gain):
    floats = hidden.astype(jnp.float32)
    factor = lax.rsqrt(lax.optimization_barrier(jnp.mean(floats * floats, axis=-1, keepdims=True)) + norm_eps)
    return (floats * factor * norm_gain.astype(jnp.float32)).astype(jnp.bfloat16)

def reference(question_hidden, recomp_hidden, norm_gain, w_query, w_keyval, pool_codes, pool_scales, block_owner, block_slot, recomp_pos):
    kv_width = KVH * HD
    normed_question = rms_rows(question_hidden, norm_gain)
    normed_recomp = rms_rows(recomp_hidden, norm_gain)
    query = jnp.dot(normed_question, w_query, preferred_element_type=jnp.float32).astype(jnp.bfloat16)
    kv_weight = w_keyval.reshape(D, 2 * kv_width)
    question_kv = jnp.dot(normed_question, kv_weight, preferred_element_type=jnp.float32).astype(jnp.bfloat16).reshape(QTOK, 2, kv_width)
    recomp_kv = jnp.dot(normed_recomp, kv_weight, preferred_element_type=jnp.float32).astype(jnp.bfloat16).reshape(RECOMP, 2, kv_width)
    pool_block = (block_owner[:, 0] * POOL_DEV + block_slot).astype(jnp.int32)
    got_codes = jnp.take(pool_codes, pool_block, axis=0).astype(jnp.float32).reshape(CTX_BLOCKS, 2, BLOCK, KVH, HD)
    got_scales = jnp.take(pool_scales, pool_block, axis=0).astype(jnp.float32)
    cached = (got_codes * got_scales[:, :, None, :, None]).astype(jnp.bfloat16)
    cached = jnp.transpose(cached.reshape(CTX_BLOCKS, 2, BLOCK, kv_width), (1, 0, 2, 3)).reshape(2, CTX_TOK, kv_width)
    kv_cache = cached.at[:, recomp_pos.astype(jnp.int32), :].set(jnp.transpose(recomp_kv, (1, 0, 2)))
    key_rows = jnp.concatenate([kv_cache[0], question_kv[:, 0]], axis=0).astype(jnp.float32)
    val_rows = jnp.concatenate([kv_cache[1], question_kv[:, 1]], axis=0).astype(jnp.float32)
    key_index = jnp.arange(CTX_TOK + QTOK, dtype=jnp.int32)
    token_index = jnp.arange(QTOK, dtype=jnp.int32)
    visible = (key_index[None, :] < CTX_TOK) | (key_index[None, :] - CTX_TOK <= token_index[:, None])
    score_scale = HD ** (-0.5)

    def one_head(head_index):
        kv_head = head_index // GROUP
        q_head = lax.dynamic_slice_in_dim(query, head_index * HD, HD, 1).astype(jnp.float32)
        k_head = lax.dynamic_slice_in_dim(key_rows, kv_head * HD, HD, 1)
        v_head = lax.dynamic_slice_in_dim(val_rows, kv_head * HD, HD, 1)
        scores = jnp.dot(q_head, k_head.T, precision=lax.Precision.HIGHEST) * score_scale
        scores = jnp.where(visible, scores, -jnp.inf)
        row_max = lax.optimization_barrier(jnp.max(scores, axis=-1, keepdims=True))
        weights = jnp.where(visible, jnp.exp(scores - row_max), 0.0)
        row_total = lax.optimization_barrier(jnp.sum(weights, axis=-1, keepdims=True))
        weights_low = lax.optimization_barrier(weights.astype(jnp.bfloat16)).astype(jnp.float32)
        summed = jnp.dot(weights_low, v_head, precision=lax.Precision.HIGHEST)
        return (summed / row_total).astype(jnp.bfloat16)
    heads = lax.map(one_head, jnp.arange(NH, dtype=jnp.int32))
    attended = jnp.transpose(heads, (1, 0, 2)).reshape(QTOK, NH * HD)
    return (attended, kv_cache)
```

```python
import functools
import math

import jax
import jax.numpy as jnp
from jax import lax
from jax.experimental import pallas as pl
from jax.experimental.pallas import tpu as pltpu
from jax.sharding import PartitionSpec as P

HD = 128
norm_eps = 1e-05
LANES = 128
VMEM = pltpu.VMEM
SMEM = pltpu.SMEM


def rms_rows(hidden, norm_gain):
    floats = hidden.astype(jnp.float32)
    factor = lax.rsqrt(jnp.mean(floats * floats, axis=-1, keepdims=True) + norm_eps)
    return (floats * factor * norm_gain.astype(jnp.float32)).astype(jnp.bfloat16)


def pick_kernel(per_dev, owner_ref, slot_ref, pool_ref, send_ref, sem):
    me = lax.axis_index("ctx")
    total_blocks = owner_ref.shape[0]

    def step(b, carry):
        count, total = carry
        dest = b // per_dev
        count = jnp.where(b % per_dev == 0, 0, count)
        mine = (owner_ref[b] == me) & (dest != me)

        @pl.when(mine)
        def _():
            pltpu.make_async_copy(
                pool_ref.at[slot_ref[b]], send_ref.at[dest, count], sem
            ).start()

        more = jnp.where(mine, 1, 0)
        return count + more, total + more

    _, total = lax.fori_loop(0, total_blocks, step, (jnp.int32(0), jnp.int32(0)))

    def drain(_, carry):
        pltpu.make_async_copy(pool_ref.at[0], send_ref.at[0, 0], sem).wait()
        return carry

    lax.fori_loop(0, total, drain, 0)


def pick_blocks(owner, slot, pool_codes, shards, capacity):
    per_dev = owner.shape[0] // shards
    return pl.pallas_call(
        functools.partial(pick_kernel, per_dev),
        out_shape=jax.ShapeDtypeStruct((shards, capacity) + pool_codes.shape[1:], pool_codes.dtype),
        in_specs=[
            pl.BlockSpec(memory_space=SMEM),
            pl.BlockSpec(memory_space=SMEM),
            pl.BlockSpec(memory_space=pl.ANY),
        ],
        out_specs=pl.BlockSpec(memory_space=pl.ANY),
        scratch_shapes=[pltpu.SemaphoreType.DMA],
        name="pick_blocks",
    )(owner, slot, pool_codes)


def attend_kernel(
    per_dev,
    kv_heads,
    owner_ref,
    slot_ref,
    scale_ref,
    pool_ref,
    codes_ref,
    query_ref,
    recomp_ref,
    own_kv_ref,
    pos_ref,
    sums_ref,
    lse_ref,
    cache_ref,
    raw,
    kv,
    tally,
    in_sem,
    out_sem,
):
    me = lax.axis_index("ctx")
    shards = codes_ref.shape[0]
    pool_dev = pool_ref.shape[0]
    block_len = pool_ref.shape[2]
    kv_width = kv_heads * HD
    tokens, q_width = query_ref.shape
    q_rows = own_kv_ref.shape[0]
    recomps = recomp_ref.shape[0]
    ctx_dev = per_dev * block_len
    group = q_width // kv_width
    base = me * per_dev

    for s in range(shards):
        tally[s] = 0

    def begin(b, carry):
        owner = owner_ref[base + b]
        rank = tally[owner]
        tally[owner] = rank + 1

        @pl.when(owner == me)
        def _():
            pltpu.make_async_copy(
                pool_ref.at[slot_ref[base + b]], raw.at[b], in_sem.at[b]
            ).start()

        @pl.when(owner != me)
        def _():
            pltpu.make_async_copy(codes_ref.at[owner, rank], raw.at[b], in_sem.at[b]).start()

        return carry

    lax.fori_loop(0, per_dev, begin, 0)

    per_chunk = math.gcd(8, per_dev)
    chunk = per_chunk * block_len

    def fill(i, carry):
        start = pl.multiple_of(i * chunk, chunk)
        local = pos_ref[...] - (me * ctx_dev + start)
        spot = lax.broadcasted_iota(jnp.int32, (chunk, recomps), 0)
        hit = jnp.where(spot == local, 1.0, 0.0).astype(jnp.float32)
        given = jnp.max(hit, axis=1, keepdims=True)
        blended = jnp.dot(
            hit.astype(jnp.bfloat16), recomp_ref[...], preferred_element_type=jnp.float32
        )
        for k in range(per_chunk):
            b = i * per_chunk + k
            pltpu.make_async_copy(pool_ref.at[0], raw.at[b], in_sem.at[b]).wait()
            at = (owner_ref[base + b] * pool_dev + slot_ref[base + b]) * (2 * kv_heads)
            rows = slice(k * block_len, (k + 1) * block_len)
            shown = given[rows] > 0.5
            for c in range(2):
                for h in range(kv_heads):
                    lanes = slice(h * HD, (h + 1) * HD)
                    wide = slice(c * kv_width + h * HD, c * kv_width + (h + 1) * HD)
                    value = raw[b, c, :, lanes].astype(jnp.float32) * scale_ref[at + c * kv_heads + h]
                    value = jnp.where(shown, blended[rows, wide], value)
                    kv[c, pl.ds(start + k * block_len, block_len), lanes] = value.astype(jnp.bfloat16)
        for c in range(2):
            pltpu.make_async_copy(
                kv.at[c, pl.ds(start, chunk)], cache_ref.at[c, pl.ds(start, chunk)], out_sem.at[i, c]
            ).start()
        return carry

    lax.fori_loop(0, per_dev // per_chunk, fill, 0)

    heads_step = math.gcd(group, max(1, 512 // tokens))
    rows = heads_step * tokens
    factor = HD ** (-0.5) * math.log2(math.e)
    lse_ref[...] = jnp.zeros_like(lse_ref)
    contract = (((1,), (1,)), ((), ()))
    lane = lax.broadcasted_iota(jnp.int32, (tokens, LANES), 1)
    row = lax.broadcasted_iota(jnp.int32, (rows, q_rows), 0)
    col = lax.broadcasted_iota(jnp.int32, (rows, q_rows), 1)
    visible = col + me * q_rows <= lax.rem(row, tokens)

    for h in range(kv_heads):
        lanes = slice(h * HD, (h + 1) * HD)
        vals = slice(kv_width + h * HD, kv_width + (h + 1) * HD)

        def one(i, carry):
            first = h * group + i * heads_step
            parts = [
                query_ref[:, pl.ds(pl.multiple_of((first + j) * HD, HD), HD)] for j in range(heads_step)
            ]
            q = parts[0] if heads_step == 1 else jnp.concatenate(parts, axis=0)
            s = lax.dot_general(q, kv[0, :, lanes], contract, preferred_element_type=jnp.float32)
            t = lax.dot_general(q, own_kv_ref[:, lanes], contract, preferred_element_type=jnp.float32)
            t = jnp.where(visible, t, -1e30)
            top = jnp.maximum(jnp.max(s, axis=1, keepdims=True), jnp.max(t, axis=1, keepdims=True))
            ps = jnp.exp2((s - top) * factor)
            pt = jnp.where(visible, jnp.exp2((t - top) * factor), 0.0)
            total = jnp.sum(ps, axis=1, keepdims=True) + jnp.sum(pt, axis=1, keepdims=True)
            o = jnp.dot(ps.astype(jnp.bfloat16), kv[1, :, lanes], preferred_element_type=jnp.float32)
            o = o + jnp.dot(
                pt.astype(jnp.bfloat16), own_kv_ref[:, vals], preferred_element_type=jnp.float32
            )
            o = o / total
            lse = top * factor + jnp.log2(total)
            for j in range(heads_step):
                here = slice(j * tokens, (j + 1) * tokens)
                sums_ref[:, pl.ds(pl.multiple_of((first + j) * HD, HD), HD)] = o[here].astype(
                    jnp.bfloat16
                )
                lse_ref[...] = jnp.where(lane == first + j, lse[here], lse_ref[...])
            return carry

        lax.fori_loop(0, group // heads_step, one, 0)

    def finish(i, carry):
        for c in range(2):
            pltpu.make_async_copy(
                kv.at[c, pl.ds(0, chunk)], cache_ref.at[c, pl.ds(0, chunk)], out_sem.at[i, c]
            ).wait()
        return carry

    lax.fori_loop(0, per_dev // per_chunk, finish, 0)


def attend(owner, slot, scales, pool_codes, got_codes, query, recomp_kv, own_kv, positions):
    shards = got_codes.shape[0]
    per_dev = owner.shape[0] // shards
    block_len, kv_width = pool_codes.shape[2:]
    tokens, q_width = query.shape
    ctx_dev = per_dev * block_len
    per_chunk = math.gcd(8, per_dev)
    smem, vmem, hbm = (pl.BlockSpec(memory_space=m) for m in (SMEM, VMEM, pl.ANY))
    return pl.pallas_call(
        functools.partial(attend_kernel, per_dev, kv_width // HD),
        out_shape=(
            jax.ShapeDtypeStruct((tokens, q_width), jnp.bfloat16),
            jax.ShapeDtypeStruct((tokens, LANES), jnp.float32),
            jax.ShapeDtypeStruct((2, ctx_dev, kv_width), jnp.bfloat16),
        ),
        in_specs=[smem, smem, smem, hbm, hbm, vmem, vmem, vmem, vmem],
        out_specs=(vmem, vmem, hbm),
        scratch_shapes=[
            VMEM((per_dev,) + pool_codes.shape[1:], jnp.bfloat16),
            VMEM((2, ctx_dev, kv_width), jnp.bfloat16),
            SMEM((shards,), jnp.int32),
            pltpu.SemaphoreType.DMA((per_dev,)),
            pltpu.SemaphoreType.DMA((per_dev // per_chunk, 2)),
        ],
        compiler_params=pltpu.CompilerParams(vmem_limit_bytes=40 * 2**20),
        name="attend",
    )(owner, slot, scales, pool_codes, got_codes, query, recomp_kv, own_kv, positions)


def body(
    question_hidden,
    recomp_hidden,
    norm_gain,
    w_query,
    w_keyval,
    pool_codes,
    pool_scales,
    block_owner,
    block_slot,
    recomp_pos,
):
    shards = lax.axis_size("ctx")
    q_rows = question_hidden.shape[0]
    r_rows = recomp_hidden.shape[0]
    row_count = q_rows + r_rows
    kv_width = w_keyval.shape[2]
    q_width = w_query.shape[1]
    heads = q_width // HD
    owner = block_owner[:, 0]
    per_dev = owner.shape[0] // shards
    capacity = max(2, 2 * per_dev // shards)

    send_codes = pick_blocks(owner, block_slot, pool_codes, shards, capacity)
    got_codes = lax.all_to_all(send_codes, "ctx", split_axis=0, concat_axis=0, tiled=True)
    scales = lax.all_gather(
        pool_scales.astype(jnp.float32).reshape(-1), "ctx", axis=0, tiled=True
    )

    normed = jnp.concatenate(
        [rms_rows(question_hidden, norm_gain), rms_rows(recomp_hidden, norm_gain)], axis=0
    )
    pieces = lax.all_to_all(normed, "ctx", split_axis=1, concat_axis=0, tiled=True)
    arranged = pieces.reshape(shards, row_count, pieces.shape[1])
    question_part = arranged[:, :q_rows, :].reshape(shards * q_rows, pieces.shape[1])
    query = lax.psum_scatter(
        jnp.dot(question_part, w_query, preferred_element_type=jnp.float32),
        "ctx",
        scatter_dimension=0,
        tiled=True,
    ).astype(jnp.bfloat16)
    kv_weight = w_keyval.reshape(w_keyval.shape[0], 2 * kv_width)
    projected = lax.psum_scatter(
        jnp.dot(pieces, kv_weight, preferred_element_type=jnp.float32),
        "ctx",
        scatter_dimension=0,
        tiled=True,
    ).astype(jnp.bfloat16)
    own_kv = projected[:q_rows]
    all_recomp = lax.all_gather(projected[q_rows:], "ctx", axis=0, tiled=True)
    every_query = lax.all_gather(query, "ctx", axis=0, tiled=True)

    sums, lse, kv_cache = attend(
        owner,
        block_slot,
        scales,
        pool_codes,
        got_codes,
        every_query,
        all_recomp,
        own_kv,
        recomp_pos.reshape(1, -1),
    )
    got_sums = lax.all_to_all(
        sums.reshape(shards, q_rows, q_width), "ctx", split_axis=0, concat_axis=0, tiled=True
    )
    got_lse = lax.all_to_all(
        lse.reshape(shards, q_rows, LANES), "ctx", split_axis=0, concat_axis=0, tiled=True
    )[:, :, :heads]
    share = jnp.exp2(got_lse - jnp.max(got_lse, axis=0))
    share = share / jnp.sum(share, axis=0)
    attended = jnp.sum(
        got_sums.reshape(shards, q_rows, heads, HD).astype(jnp.float32) * share[..., None], axis=0
    )
    return (attended.reshape(q_rows, q_width).astype(jnp.bfloat16), kv_cache)


def solution(mesh):
    placed = (
        P(("groups", "ctx"), None),
        P(("groups", "ctx"), None),
        P(),
        P("ctx", "tp"),
        P("ctx", None, "tp"),
        P(("groups", "ctx"), None, None, "tp"),
        P(("groups", "ctx"), None, "tp"),
        P("groups", None),
        P("groups"),
        P("groups"),
    )
    return jax.shard_map(
        body,
        mesh=mesh,
        in_specs=placed,
        out_specs=(P(("groups", "ctx"), "tp"), P(None, ("groups", "ctx"), "tp")),
        check_vma=False,
    )
```

```python
import functools
import math

import jax
import jax.numpy as jnp
from jax import lax
from jax.experimental import pallas as pl
from jax.experimental.pallas import tpu as pltpu
from jax.sharding import PartitionSpec as P

HD = 128
norm_eps = 1e-05
LANES = 128
VMEM = pltpu.VMEM
SMEM = pltpu.SMEM


def rms_rows(hidden, norm_gain):
    floats = hidden.astype(jnp.float32)
    factor = lax.rsqrt(jnp.mean(floats * floats, axis=-1, keepdims=True) + norm_eps)
    return (floats * factor * norm_gain.astype(jnp.float32)).astype(jnp.bfloat16)


def attend_kernel(
    per_dev,
    kv_heads,
    owner_ref,
    slot_ref,
    scale_ref,
    pool_ref,
    codes_ref,
    query_ref,
    recomp_ref,
    own_kv_ref,
    pos_ref,
    sums_ref,
    cache_ref,
    raw,
    kv,
    lse_ref,
    tally,
    in_sem,
    out_sem,
):
    me = lax.axis_index("ctx")
    shards = codes_ref.shape[0]
    pool_dev = pool_ref.shape[0]
    block_len = pool_ref.shape[2]
    kv_width = kv_heads * HD
    tokens, q_width = query_ref.shape
    q_rows = own_kv_ref.shape[0]
    recomps = recomp_ref.shape[0]
    ctx_dev = per_dev * block_len
    group = q_width // kv_width
    base = me * per_dev

    for s in range(shards):
        tally[s] = 0

    def begin(b, carry):
        owner = owner_ref[base + b]
        rank = tally[owner]
        tally[owner] = rank + 1

        @pl.when(owner == me)
        def _():
            pltpu.make_async_copy(
                pool_ref.at[slot_ref[base + b]], raw.at[b], in_sem.at[b]
            ).start()

        @pl.when(owner != me)
        def _():
            pltpu.make_async_copy(codes_ref.at[owner, rank], raw.at[b], in_sem.at[b]).start()

        return carry

    lax.fori_loop(0, per_dev, begin, 0)

    per_chunk = math.gcd(8, per_dev)
    chunk = per_chunk * block_len

    def fill(i, carry):
        start = pl.multiple_of(i * chunk, chunk)
        local = pos_ref[...] - (me * ctx_dev + start)
        spot = lax.broadcasted_iota(jnp.int32, (chunk, recomps), 0)
        hit = jnp.where(spot == local, 1.0, 0.0).astype(jnp.float32)
        given = jnp.max(hit, axis=1, keepdims=True)
        blended = jnp.dot(
            hit.astype(jnp.bfloat16), recomp_ref[...], preferred_element_type=jnp.float32
        )
        for k in range(per_chunk):
            b = i * per_chunk + k
            pltpu.make_async_copy(pool_ref.at[0], raw.at[b], in_sem.at[b]).wait()
            at = (owner_ref[base + b] * pool_dev + slot_ref[base + b]) * (2 * kv_heads)
            rows = slice(k * block_len, (k + 1) * block_len)
            shown = given[rows] > 0.5
            for c in range(2):
                for h in range(kv_heads):
                    lanes = slice(h * HD, (h + 1) * HD)
                    wide = slice(c * kv_width + h * HD, c * kv_width + (h + 1) * HD)
                    value = raw[b, c, :, lanes].astype(jnp.float32) * scale_ref[at + c * kv_heads + h]
                    value = jnp.where(shown, blended[rows, wide], value)
                    kv[c, pl.ds(start + k * block_len, block_len), lanes] = value.astype(jnp.bfloat16)
        for c in range(2):
            pltpu.make_async_copy(
                kv.at[c, pl.ds(start, chunk)], cache_ref.at[c, pl.ds(start, chunk)], out_sem.at[i, c]
            ).start()
        return carry

    lax.fori_loop(0, per_dev // per_chunk, fill, 0)

    heads_step = math.gcd(group, max(1, 512 // tokens))
    rows = heads_step * tokens
    factor = HD ** (-0.5) * math.log2(math.e)
    lse_ref[...] = jnp.zeros_like(lse_ref)
    contract = (((1,), (1,)), ((), ()))
    lane = lax.broadcasted_iota(jnp.int32, (tokens, LANES), 1)
    row = lax.broadcasted_iota(jnp.int32, (rows, q_rows), 0)
    col = lax.broadcasted_iota(jnp.int32, (rows, q_rows), 1)
    visible = col + me * q_rows <= lax.rem(row, tokens)

    for h in range(kv_heads):
        lanes = slice(h * HD, (h + 1) * HD)
        vals = slice(kv_width + h * HD, kv_width + (h + 1) * HD)

        def one(i, carry):
            first = h * group + i * heads_step
            parts = [
                query_ref[:, pl.ds(pl.multiple_of((first + j) * HD, HD), HD)] for j in range(heads_step)
            ]
            q = parts[0] if heads_step == 1 else jnp.concatenate(parts, axis=0)
            s = lax.dot_general(q, kv[0, :, lanes], contract, preferred_element_type=jnp.float32)
            t = lax.dot_general(q, own_kv_ref[:, lanes], contract, preferred_element_type=jnp.float32)
            t = jnp.where(visible, t, -1e30)
            top = jnp.maximum(jnp.max(s, axis=1, keepdims=True), jnp.max(t, axis=1, keepdims=True))
            ps = jnp.exp2((s - top) * factor)
            pt = jnp.where(visible, jnp.exp2((t - top) * factor), 0.0)
            total = jnp.sum(ps, axis=1, keepdims=True) + jnp.sum(pt, axis=1, keepdims=True)
            o = jnp.dot(ps.astype(jnp.bfloat16), kv[1, :, lanes], preferred_element_type=jnp.float32)
            o = o + jnp.dot(
                pt.astype(jnp.bfloat16), own_kv_ref[:, vals], preferred_element_type=jnp.float32
            )
            o = o / total
            lse = top * factor + jnp.log2(total)
            for j in range(heads_step):
                here = slice(j * tokens, (j + 1) * tokens)
                sums_ref[:, pl.ds(pl.multiple_of((first + j) * HD, HD), HD)] = o[here].astype(
                    jnp.bfloat16
                )
                lse_ref[...] = jnp.where(lane == first + j, lse[here], lse_ref[...])
            return carry

        lax.fori_loop(0, group // heads_step, one, 0)

    rest = lse_ref[...]
    for k in range(3):
        term = rest.astype(jnp.bfloat16)
        sums_ref[:, q_width + k * LANES : q_width + (k + 1) * LANES] = term
        rest = rest - term.astype(jnp.float32)

    def finish(i, carry):
        for c in range(2):
            pltpu.make_async_copy(
                kv.at[c, pl.ds(0, chunk)], cache_ref.at[c, pl.ds(0, chunk)], out_sem.at[i, c]
            ).wait()
        return carry

    lax.fori_loop(0, per_dev // per_chunk, finish, 0)


def attend(owner, slot, scales, pool_codes, got_codes, query, recomp_kv, own_kv, positions):
    shards = got_codes.shape[0]
    per_dev = owner.shape[0] // shards
    block_len, kv_width = pool_codes.shape[2:]
    tokens, q_width = query.shape
    ctx_dev = per_dev * block_len
    per_chunk = math.gcd(8, per_dev)
    smem, vmem, hbm = (pl.BlockSpec(memory_space=m) for m in (SMEM, VMEM, pl.ANY))
    return pl.pallas_call(
        functools.partial(attend_kernel, per_dev, kv_width // HD),
        out_shape=(
            jax.ShapeDtypeStruct((tokens, q_width + 3 * LANES), jnp.bfloat16),
            jax.ShapeDtypeStruct((2, ctx_dev, kv_width), jnp.bfloat16),
        ),
        in_specs=[smem, smem, smem, hbm, hbm, vmem, vmem, vmem, vmem],
        out_specs=(vmem, hbm),
        scratch_shapes=[
            VMEM((per_dev,) + pool_codes.shape[1:], jnp.bfloat16),
            VMEM((2, ctx_dev, kv_width), jnp.bfloat16),
            VMEM((tokens, LANES), jnp.float32),
            SMEM((shards,), jnp.int32),
            pltpu.SemaphoreType.DMA((per_dev,)),
            pltpu.SemaphoreType.DMA((per_dev // per_chunk, 2)),
        ],
        compiler_params=pltpu.CompilerParams(vmem_limit_bytes=40 * 2**20),
        name="attend",
    )(owner, slot, scales, pool_codes, got_codes, query, recomp_kv, own_kv, positions)


def body(
    question_hidden,
    recomp_hidden,
    norm_gain,
    w_query,
    w_keyval,
    pool_codes,
    pool_scales,
    block_owner,
    block_slot,
    recomp_pos,
):
    shards = lax.axis_size("ctx")
    q_rows = question_hidden.shape[0]
    r_rows = recomp_hidden.shape[0]
    row_count = q_rows + r_rows
    kv_width = w_keyval.shape[2]
    q_width = w_query.shape[1]
    heads = q_width // HD
    owner = block_owner[:, 0]
    per_dev = owner.shape[0] // shards
    capacity = max(2, 2 * per_dev // shards)

    own_index = lax.axis_index("ctx")
    owners = owner.reshape(shards, per_dev)
    positions = jnp.arange(per_dev)
    earlier = positions[None, :] < positions[:, None]
    same = owners[:, :, None] == owners[:, None, :]
    rank = jnp.sum((same & earlier[None]).astype(jnp.int32), axis=2)
    chosen = (owners == own_index)[:, :, None] & (
        rank[:, :, None] == jnp.arange(capacity)[None, None, :]
    )
    send_slot = jnp.sum(
        jnp.where(chosen, block_slot.reshape(shards, per_dev)[:, :, None], 0), axis=1
    ).reshape(-1)
    send_codes = pool_codes.at[send_slot].get(mode="promise_in_bounds")
    send_codes = send_codes.reshape((shards, capacity) + pool_codes.shape[1:])
    got_codes = lax.all_to_all(send_codes, "ctx", split_axis=0, concat_axis=0, tiled=True)

    normed = jnp.concatenate(
        [rms_rows(question_hidden, norm_gain), rms_rows(recomp_hidden, norm_gain)], axis=0
    )
    pieces = lax.all_to_all(normed, "ctx", split_axis=1, concat_axis=0, tiled=True)
    arranged = pieces.reshape(shards, row_count, pieces.shape[1])
    question_part = arranged[:, :q_rows, :].reshape(shards * q_rows, pieces.shape[1])
    query = lax.psum_scatter(
        jnp.dot(question_part, w_query, preferred_element_type=jnp.float32),
        "ctx",
        scatter_dimension=0,
        tiled=True,
    ).astype(jnp.bfloat16)
    kv_weight = w_keyval.reshape(w_keyval.shape[0], 2 * kv_width)
    projected = lax.psum_scatter(
        jnp.dot(pieces, kv_weight, preferred_element_type=jnp.float32),
        "ctx",
        scatter_dimension=0,
        tiled=True,
    ).astype(jnp.bfloat16)
    own_kv = projected[:q_rows]
    extra = 16
    scale_count = pool_scales.size
    scale_rows = jnp.pad(
        pool_scales.reshape(1, -1), ((0, extra - 1), (0, 2 * kv_width - scale_count))
    )
    shared = lax.all_gather(
        jnp.concatenate([projected[q_rows:], scale_rows], axis=0), "ctx", axis=0, tiled=True
    )
    scales = (
        shared.reshape(shards, r_rows + extra, 2 * kv_width)[:, r_rows, :scale_count]
        .astype(jnp.float32)
        .reshape(-1)
    )
    where_to = jnp.pad(
        recomp_pos.reshape(shards, r_rows), ((0, 0), (0, extra)), constant_values=-1
    ).reshape(1, -1)
    every_query = lax.all_gather(query, "ctx", axis=0, tiled=True)

    sums, kv_cache = attend(
        owner,
        block_slot,
        scales,
        pool_codes,
        got_codes,
        every_query,
        shared,
        own_kv,
        where_to,
    )
    got = lax.all_to_all(
        sums.reshape(shards, q_rows, sums.shape[1]), "ctx", split_axis=0, concat_axis=0, tiled=True
    )
    terms = got[:, :, q_width:].astype(jnp.float32).reshape(shards, q_rows, 3, LANES)[..., :heads]
    got_lse = terms[:, :, 0] + terms[:, :, 1] + terms[:, :, 2]
    got_sums = got[:, :, :q_width]
    share = jnp.exp2(got_lse - jnp.max(got_lse, axis=0))
    share = share / jnp.sum(share, axis=0)
    attended = jnp.sum(
        got_sums.reshape(shards, q_rows, heads, HD).astype(jnp.float32) * share[..., None], axis=0
    )
    return (attended.reshape(q_rows, q_width).astype(jnp.bfloat16), kv_cache)


def solution(mesh):
    placed = (
        P(("groups", "ctx"), None),
        P(("groups", "ctx"), None),
        P(),
        P("ctx", "tp"),
        P("ctx", None, "tp"),
        P(("groups", "ctx"), None, None, "tp"),
        P(("groups", "ctx"), None, "tp"),
        P("groups", None),
        P("groups"),
        P("groups"),
    )
    return jax.shard_map(
        body,
        mesh=mesh,
        in_specs=placed,
        out_specs=(P(("groups", "ctx"), "tp"), P(None, ("groups", "ctx"), "tp")),
        check_vma=False,
    )
```

```python
import functools
import math

import jax
import jax.numpy as jnp
from jax import lax
from jax.experimental import pallas as pl
from jax.experimental.pallas import tpu as pltpu
from jax.sharding import PartitionSpec as P

HD = 128
norm_eps = 1e-05
LANES = 128
VMEM = pltpu.VMEM
SMEM = pltpu.SMEM


def rms_rows(hidden, norm_gain):
    floats = hidden.astype(jnp.float32)
    factor = lax.rsqrt(jnp.mean(floats * floats, axis=-1, keepdims=True) + norm_eps)
    return (floats * factor * norm_gain.astype(jnp.float32)).astype(jnp.bfloat16)


def attend_kernel(
    per_dev,
    kv_heads,
    shards,
    owner_ref,
    slot_ref,
    scale_ref,
    pool_ref,
    *refs,
):
    got_refs = refs[: shards - 1]
    attend_body(
        per_dev, kv_heads, shards, owner_ref, slot_ref, scale_ref, pool_ref, got_refs, *refs[shards - 1 :]
    )


def attend_body(
    per_dev,
    kv_heads,
    shards,
    owner_ref,
    slot_ref,
    scale_ref,
    pool_ref,
    got_refs,
    query_ref,
    recomp_ref,
    own_kv_ref,
    pos_ref,
    sums_ref,
    cache_ref,
    raw,
    kv,
    lse_ref,
    tally,
    in_sem,
    out_sem,
):
    me = lax.axis_index("ctx")
    pool_dev = pool_ref.shape[0]
    block_len = pool_ref.shape[2]
    kv_width = kv_heads * HD
    tokens, q_width = query_ref.shape
    q_rows = own_kv_ref.shape[0]
    recomps = recomp_ref.shape[0]
    ctx_dev = per_dev * block_len
    group = q_width // kv_width
    base = me * per_dev

    for s in range(shards):
        tally[s] = 0

    def begin(b, carry):
        owner = owner_ref[base + b]
        rank = tally[owner]
        tally[owner] = rank + 1

        @pl.when(owner == me)
        def _():
            pltpu.make_async_copy(
                pool_ref.at[slot_ref[base + b]], raw.at[b], in_sem.at[b]
            ).start()

        for shift in range(1, shards):

            @pl.when(owner == lax.rem(me + shards - shift, shards))
            def _(shift=shift):
                pltpu.make_async_copy(
                    got_refs[shift - 1].at[rank], raw.at[b], in_sem.at[b]
                ).start()

        return carry

    lax.fori_loop(0, per_dev, begin, 0)

    per_chunk = math.gcd(8, per_dev)
    chunk = per_chunk * block_len

    def fill(i, carry):
        start = pl.multiple_of(i * chunk, chunk)
        local = pos_ref[...] - (me * ctx_dev + start)
        spot = lax.broadcasted_iota(jnp.int32, (chunk, recomps), 0)
        hit = jnp.where(spot == local, 1.0, 0.0).astype(jnp.float32)
        given = jnp.max(hit, axis=1, keepdims=True)
        blended = jnp.dot(
            hit.astype(jnp.bfloat16), recomp_ref[...], preferred_element_type=jnp.float32
        )
        for k in range(per_chunk):
            b = i * per_chunk + k
            pltpu.make_async_copy(pool_ref.at[0], raw.at[b], in_sem.at[b]).wait()
            at = (owner_ref[base + b] * pool_dev + slot_ref[base + b]) * (2 * kv_heads)
            rows = slice(k * block_len, (k + 1) * block_len)
            shown = given[rows] > 0.5
            for c in range(2):
                for h in range(kv_heads):
                    lanes = slice(h * HD, (h + 1) * HD)
                    wide = slice(c * kv_width + h * HD, c * kv_width + (h + 1) * HD)
                    value = raw[b, c, :, lanes].astype(jnp.float32) * scale_ref[at + c * kv_heads + h]
                    value = jnp.where(shown, blended[rows, wide], value)
                    kv[c, pl.ds(start + k * block_len, block_len), lanes] = value.astype(jnp.bfloat16)
        for c in range(2):
            pltpu.make_async_copy(
                kv.at[c, pl.ds(start, chunk)], cache_ref.at[c, pl.ds(start, chunk)], out_sem.at[i, c]
            ).start()
        return carry

    lax.fori_loop(0, per_dev // per_chunk, fill, 0)

    heads_step = math.gcd(group, max(1, 512 // tokens))
    rows = heads_step * tokens
    factor = HD ** (-0.5) * math.log2(math.e)
    lse_ref[...] = jnp.zeros_like(lse_ref)
    contract = (((1,), (1,)), ((), ()))
    lane = lax.broadcasted_iota(jnp.int32, (tokens, LANES), 1)
    row = lax.broadcasted_iota(jnp.int32, (rows, q_rows), 0)
    col = lax.broadcasted_iota(jnp.int32, (rows, q_rows), 1)
    visible = col + me * q_rows <= lax.rem(row, tokens)

    for h in range(kv_heads):
        lanes = slice(h * HD, (h + 1) * HD)
        vals = slice(kv_width + h * HD, kv_width + (h + 1) * HD)

        def one(i, carry):
            first = h * group + i * heads_step
            parts = [
                query_ref[:, pl.ds(pl.multiple_of((first + j) * HD, HD), HD)] for j in range(heads_step)
            ]
            q = parts[0] if heads_step == 1 else jnp.concatenate(parts, axis=0)
            s = lax.dot_general(q, kv[0, :, lanes], contract, preferred_element_type=jnp.float32)
            t = lax.dot_general(q, own_kv_ref[:, lanes], contract, preferred_element_type=jnp.float32)
            t = jnp.where(visible, t, -1e30)
            top = jnp.maximum(jnp.max(s, axis=1, keepdims=True), jnp.max(t, axis=1, keepdims=True))
            ps = jnp.exp2((s - top) * factor)
            pt = jnp.where(visible, jnp.exp2((t - top) * factor), 0.0)
            total = jnp.sum(ps, axis=1, keepdims=True) + jnp.sum(pt, axis=1, keepdims=True)
            o = jnp.dot(ps.astype(jnp.bfloat16), kv[1, :, lanes], preferred_element_type=jnp.float32)
            o = o + jnp.dot(
                pt.astype(jnp.bfloat16), own_kv_ref[:, vals], preferred_element_type=jnp.float32
            )
            o = o / total
            lse = top * factor + jnp.log2(total)
            for j in range(heads_step):
                here = slice(j * tokens, (j + 1) * tokens)
                sums_ref[:, pl.ds(pl.multiple_of((first + j) * HD, HD), HD)] = o[here].astype(
                    jnp.bfloat16
                )
                lse_ref[...] = jnp.where(lane == first + j, lse[here], lse_ref[...])
            return carry

        lax.fori_loop(0, group // heads_step, one, 0)

    rest = lse_ref[...]
    for k in range(3):
        term = rest.astype(jnp.bfloat16)
        sums_ref[:, q_width + k * LANES : q_width + (k + 1) * LANES] = term
        rest = rest - term.astype(jnp.float32)

    def finish(i, carry):
        for c in range(2):
            pltpu.make_async_copy(
                kv.at[c, pl.ds(0, chunk)], cache_ref.at[c, pl.ds(0, chunk)], out_sem.at[i, c]
            ).wait()
        return carry

    lax.fori_loop(0, per_dev // per_chunk, finish, 0)


def attend(owner, slot, scales, pool_codes, got_codes, query, recomp_kv, own_kv, positions):
    shards = len(got_codes) + 1
    per_dev = owner.shape[0] // shards
    block_len, kv_width = pool_codes.shape[2:]
    tokens, q_width = query.shape
    ctx_dev = per_dev * block_len
    per_chunk = math.gcd(8, per_dev)
    smem, vmem, hbm = (pl.BlockSpec(memory_space=m) for m in (SMEM, VMEM, pl.ANY))
    return pl.pallas_call(
        functools.partial(attend_kernel, per_dev, kv_width // HD, shards),
        out_shape=(
            jax.ShapeDtypeStruct((tokens, q_width + 3 * LANES), jnp.bfloat16),
            jax.ShapeDtypeStruct((2, ctx_dev, kv_width), jnp.bfloat16),
        ),
        in_specs=[smem, smem, smem] + [hbm] * shards + [vmem, vmem, vmem, vmem],
        out_specs=(vmem, hbm),
        scratch_shapes=[
            VMEM((per_dev,) + pool_codes.shape[1:], jnp.bfloat16),
            VMEM((2, ctx_dev, kv_width), jnp.bfloat16),
            VMEM((tokens, LANES), jnp.float32),
            SMEM((shards,), jnp.int32),
            pltpu.SemaphoreType.DMA((per_dev,)),
            pltpu.SemaphoreType.DMA((per_dev // per_chunk, 2)),
        ],
        compiler_params=pltpu.CompilerParams(vmem_limit_bytes=40 * 2**20),
        name="attend",
    )(owner, slot, scales, pool_codes, *got_codes, query, recomp_kv, own_kv, positions)


def body(
    question_hidden,
    recomp_hidden,
    norm_gain,
    w_query,
    w_keyval,
    pool_codes,
    pool_scales,
    block_owner,
    block_slot,
    recomp_pos,
):
    shards = lax.axis_size("ctx")
    q_rows = question_hidden.shape[0]
    r_rows = recomp_hidden.shape[0]
    row_count = q_rows + r_rows
    kv_width = w_keyval.shape[2]
    q_width = w_query.shape[1]
    heads = q_width // HD
    owner = block_owner[:, 0]
    per_dev = owner.shape[0] // shards
    capacity = max(2, 2 * per_dev // shards)

    own_index = lax.axis_index("ctx")
    owners = owner.reshape(shards, per_dev)
    positions = jnp.arange(per_dev)
    earlier = positions[None, :] < positions[:, None]
    same = owners[:, :, None] == owners[:, None, :]
    rank = jnp.sum((same & earlier[None]).astype(jnp.int32), axis=2)
    chosen = (owners == own_index)[:, :, None] & (
        rank[:, :, None] == jnp.arange(capacity)[None, None, :]
    )
    send_slot = jnp.sum(
        jnp.where(chosen, block_slot.reshape(shards, per_dev)[:, :, None], 0), axis=1
    )
    got_codes = []
    for shift in range(1, shards):
        wanted = lax.dynamic_index_in_dim(
            send_slot, lax.rem(own_index + shift, shards), 0, keepdims=False
        )
        blocks = pool_codes.at[wanted].get(mode="promise_in_bounds")
        pairs = [(i, (i + shift) % shards) for i in range(shards)]
        got_codes.append(lax.ppermute(blocks, "ctx", pairs))

    normed = jnp.concatenate(
        [rms_rows(question_hidden, norm_gain), rms_rows(recomp_hidden, norm_gain)], axis=0
    )
    pieces = lax.all_to_all(normed, "ctx", split_axis=1, concat_axis=0, tiled=True)
    arranged = pieces.reshape(shards, row_count, pieces.shape[1])
    question_part = arranged[:, :q_rows, :].reshape(shards * q_rows, pieces.shape[1])
    query = lax.psum_scatter(
        jnp.dot(question_part, w_query, preferred_element_type=jnp.float32),
        "ctx",
        scatter_dimension=0,
        tiled=True,
    ).astype(jnp.bfloat16)
    kv_weight = w_keyval.reshape(w_keyval.shape[0], 2 * kv_width)
    projected = lax.psum_scatter(
        jnp.dot(pieces, kv_weight, preferred_element_type=jnp.float32),
        "ctx",
        scatter_dimension=0,
        tiled=True,
    ).astype(jnp.bfloat16)
    own_kv = projected[:q_rows]
    extra = 16
    scale_count = pool_scales.size
    scale_rows = jnp.pad(
        pool_scales.reshape(1, -1), ((0, extra - 1), (0, 2 * kv_width - scale_count))
    )
    shared = lax.all_gather(
        jnp.concatenate([projected[q_rows:], scale_rows], axis=0), "ctx", axis=0, tiled=True
    )
    scales = (
        shared.reshape(shards, r_rows + extra, 2 * kv_width)[:, r_rows, :scale_count]
        .astype(jnp.float32)
        .reshape(-1)
    )
    where_to = jnp.pad(
        recomp_pos.reshape(shards, r_rows), ((0, 0), (0, extra)), constant_values=-1
    ).reshape(1, -1)
    every_query = lax.all_gather(query, "ctx", axis=0, tiled=True)

    sums, kv_cache = attend(
        owner,
        block_slot,
        scales,
        pool_codes,
        got_codes,
        every_query,
        shared,
        own_kv,
        where_to,
    )
    got = lax.all_to_all(
        sums.reshape(shards, q_rows, sums.shape[1]), "ctx", split_axis=0, concat_axis=0, tiled=True
    )
    terms = got[:, :, q_width:].astype(jnp.float32).reshape(shards, q_rows, 3, LANES)[..., :heads]
    got_lse = terms[:, :, 0] + terms[:, :, 1] + terms[:, :, 2]
    got_sums = got[:, :, :q_width]
    share = jnp.exp2(got_lse - jnp.max(got_lse, axis=0))
    share = share / jnp.sum(share, axis=0)
    attended = jnp.sum(
        got_sums.reshape(shards, q_rows, heads, HD).astype(jnp.float32) * share[..., None], axis=0
    )
    return (attended.reshape(q_rows, q_width).astype(jnp.bfloat16), kv_cache)


def solution(mesh):
    placed = (
        P(("groups", "ctx"), None),
        P(("groups", "ctx"), None),
        P(),
        P("ctx", "tp"),
        P("ctx", None, "tp"),
        P(("groups", "ctx"), None, None, "tp"),
        P(("groups", "ctx"), None, "tp"),
        P("groups", None),
        P("groups"),
        P("groups"),
    )
    return jax.shard_map(
        body,
        mesh=mesh,
        in_specs=placed,
        out_specs=(P(("groups", "ctx"), "tp"), P(None, ("groups", "ctx"), "tp")),
        check_vma=False,
    )
```

```python
import functools
import math

import jax
import jax.numpy as jnp
from jax import lax
from jax.experimental import pallas as pl
from jax.experimental.pallas import tpu as pltpu
from jax.sharding import PartitionSpec as P

HD = 128
norm_eps = 1e-05
LANES = 128
VMEM = pltpu.VMEM
SMEM = pltpu.SMEM


def rms_rows(hidden, norm_gain):
    floats = hidden.astype(jnp.float32)
    factor = lax.rsqrt(jnp.mean(floats * floats, axis=-1, keepdims=True) + norm_eps)
    return (floats * factor * norm_gain.astype(jnp.float32)).astype(jnp.bfloat16)


def attend_kernel(
    per_dev,
    kv_heads,
    shards,
    owner_ref,
    slot_ref,
    scale_ref,
    pool_ref,
    *refs,
):
    got_refs = refs[: shards - 1]
    attend_body(
        per_dev, kv_heads, shards, owner_ref, slot_ref, scale_ref, pool_ref, got_refs, *refs[shards - 1 :]
    )


def attend_body(
    per_dev,
    kv_heads,
    shards,
    owner_ref,
    slot_ref,
    scale_ref,
    pool_ref,
    got_refs,
    query_ref,
    recomp_ref,
    own_kv_ref,
    pos_ref,
    sums_ref,
    cache_ref,
    raw,
    kv,
    lse_ref,
    tally,
    in_sem,
    out_sem,
):
    me = lax.axis_index("ctx")
    pool_dev = pool_ref.shape[0]
    block_len = pool_ref.shape[2]
    kv_width = kv_heads * HD
    tokens, q_width = query_ref.shape
    q_rows = own_kv_ref.shape[0]
    recomps = recomp_ref.shape[0]
    ctx_dev = per_dev * block_len
    group = q_width // kv_width
    base = me * per_dev

    for s in range(shards):
        tally[s] = 0

    def begin(b, carry):
        owner = owner_ref[base + b]
        rank = tally[owner]
        tally[owner] = rank + 1

        @pl.when(owner == me)
        def _():
            pltpu.make_async_copy(
                pool_ref.at[slot_ref[base + b]], raw.at[b], in_sem.at[b]
            ).start()

        for shift in range(1, shards):

            @pl.when(owner == lax.rem(me + shards - shift, shards))
            def _(shift=shift):
                pltpu.make_async_copy(
                    got_refs[shift - 1].at[rank], raw.at[b], in_sem.at[b]
                ).start()

        return carry

    lax.fori_loop(0, per_dev, begin, 0)

    per_chunk = math.gcd(8, per_dev)
    chunk = per_chunk * block_len

    def fill(i, carry):
        start = pl.multiple_of(i * chunk, chunk)
        local = pos_ref[...] - (me * ctx_dev + start)
        spot = lax.broadcasted_iota(jnp.int32, (chunk, recomps), 0)
        hit = jnp.where(spot == local, 1.0, 0.0).astype(jnp.float32)
        given = jnp.max(hit, axis=1, keepdims=True)
        blended = jnp.dot(
            hit.astype(jnp.bfloat16), recomp_ref[...], preferred_element_type=jnp.float32
        )
        for k in range(per_chunk):
            b = i * per_chunk + k
            pltpu.make_async_copy(pool_ref.at[0], raw.at[b], in_sem.at[b]).wait()
            at = (owner_ref[base + b] * pool_dev + slot_ref[base + b]) * (2 * kv_heads)
            rows = slice(k * block_len, (k + 1) * block_len)
            shown = given[rows] > 0.5
            for c in range(2):
                for h in range(kv_heads):
                    lanes = slice(h * HD, (h + 1) * HD)
                    wide = slice(c * kv_width + h * HD, c * kv_width + (h + 1) * HD)
                    value = raw[b, c, :, lanes].astype(jnp.float32) * scale_ref[at + c * kv_heads + h]
                    value = jnp.where(shown, blended[rows, wide], value)
                    kv[c, pl.ds(start + k * block_len, block_len), lanes] = value.astype(jnp.bfloat16)
        for c in range(2):
            pltpu.make_async_copy(
                kv.at[c, pl.ds(start, chunk)], cache_ref.at[c, pl.ds(start, chunk)], out_sem.at[i, c]
            ).start()
        return carry

    lax.fori_loop(0, per_dev // per_chunk, fill, 0)

    heads_step = math.gcd(group, max(1, 512 // tokens))
    rows = heads_step * tokens
    factor = HD ** (-0.5) * math.log2(math.e)
    lse_ref[...] = jnp.zeros_like(lse_ref)
    contract = (((1,), (1,)), ((), ()))
    lane = lax.broadcasted_iota(jnp.int32, (tokens, LANES), 1)
    row = lax.broadcasted_iota(jnp.int32, (rows, q_rows), 0)
    col = lax.broadcasted_iota(jnp.int32, (rows, q_rows), 1)
    visible = col + me * q_rows <= lax.rem(row, tokens)

    for h in range(kv_heads):
        lanes = slice(h * HD, (h + 1) * HD)
        vals = slice(kv_width + h * HD, kv_width + (h + 1) * HD)

        def one(i, carry):
            first = h * group + i * heads_step
            parts = [
                query_ref[:, pl.ds(pl.multiple_of((first + j) * HD, HD), HD)] for j in range(heads_step)
            ]
            q = parts[0] if heads_step == 1 else jnp.concatenate(parts, axis=0)
            s = lax.dot_general(q, kv[0, :, lanes], contract, preferred_element_type=jnp.float32)
            t = lax.dot_general(q, own_kv_ref[:, lanes], contract, preferred_element_type=jnp.float32)
            t = jnp.where(visible, t, -1e30)
            top = jnp.maximum(jnp.max(s, axis=1, keepdims=True), jnp.max(t, axis=1, keepdims=True))
            ps = jnp.exp2((s - top) * factor)
            pt = jnp.where(visible, jnp.exp2((t - top) * factor), 0.0)
            total = jnp.sum(ps, axis=1, keepdims=True) + jnp.sum(pt, axis=1, keepdims=True)
            o = jnp.dot(ps.astype(jnp.bfloat16), kv[1, :, lanes], preferred_element_type=jnp.float32)
            o = o + jnp.dot(
                pt.astype(jnp.bfloat16), own_kv_ref[:, vals], preferred_element_type=jnp.float32
            )
            o = o / total
            lse = top * factor + jnp.log2(total)
            for j in range(heads_step):
                here = slice(j * tokens, (j + 1) * tokens)
                sums_ref[:, pl.ds(pl.multiple_of((first + j) * HD, HD), HD)] = o[here].astype(
                    jnp.bfloat16
                )
                lse_ref[...] = jnp.where(lane == first + j, lse[here], lse_ref[...])
            return carry

        lax.fori_loop(0, group // heads_step, one, 0)

    rest = lse_ref[...]
    for k in range(3):
        term = rest.astype(jnp.bfloat16)
        sums_ref[:, q_width + k * LANES : q_width + (k + 1) * LANES] = term
        rest = rest - term.astype(jnp.float32)

    def finish(i, carry):
        for c in range(2):
            pltpu.make_async_copy(
                kv.at[c, pl.ds(0, chunk)], cache_ref.at[c, pl.ds(0, chunk)], out_sem.at[i, c]
            ).wait()
        return carry

    lax.fori_loop(0, per_dev // per_chunk, finish, 0)


def attend(owner, slot, scales, pool_codes, got_codes, query, recomp_kv, own_kv, positions):
    shards = len(got_codes) + 1
    per_dev = owner.shape[0] // shards
    block_len, kv_width = pool_codes.shape[2:]
    tokens, q_width = query.shape
    ctx_dev = per_dev * block_len
    per_chunk = math.gcd(8, per_dev)
    smem, vmem, hbm = (pl.BlockSpec(memory_space=m) for m in (SMEM, VMEM, pl.ANY))
    return pl.pallas_call(
        functools.partial(attend_kernel, per_dev, kv_width // HD, shards),
        out_shape=(
            jax.ShapeDtypeStruct((tokens, q_width + 3 * LANES), jnp.bfloat16),
            jax.ShapeDtypeStruct((2, ctx_dev, kv_width), jnp.bfloat16),
        ),
        in_specs=[smem, smem, smem] + [hbm] * shards + [vmem, vmem, vmem, vmem],
        out_specs=(vmem, hbm),
        scratch_shapes=[
            VMEM((per_dev,) + pool_codes.shape[1:], jnp.bfloat16),
            VMEM((2, ctx_dev, kv_width), jnp.bfloat16),
            VMEM((tokens, LANES), jnp.float32),
            SMEM((shards,), jnp.int32),
            pltpu.SemaphoreType.DMA((per_dev,)),
            pltpu.SemaphoreType.DMA((per_dev // per_chunk, 2)),
        ],
        compiler_params=pltpu.CompilerParams(vmem_limit_bytes=40 * 2**20),
        name="attend",
    )(owner, slot, scales, pool_codes, *got_codes, query, recomp_kv, own_kv, positions)


def body(
    question_hidden,
    recomp_hidden,
    norm_gain,
    w_query,
    w_keyval,
    pool_codes,
    pool_scales,
    block_owner,
    block_slot,
    recomp_pos,
):
    shards = lax.axis_size("ctx")
    q_rows = question_hidden.shape[0]
    r_rows = recomp_hidden.shape[0]
    row_count = q_rows + r_rows
    kv_width = w_keyval.shape[2]
    q_width = w_query.shape[1]
    heads = q_width // HD
    owner = block_owner[:, 0]
    per_dev = owner.shape[0] // shards
    capacity = max(2, 2 * per_dev // shards)

    own_index = lax.axis_index("ctx")
    owners = owner.reshape(shards, per_dev)
    positions = jnp.arange(per_dev)
    earlier = positions[None, :] < positions[:, None]
    same = owners[:, :, None] == owners[:, None, :]
    rank = jnp.sum((same & earlier[None]).astype(jnp.int32), axis=2)
    chosen = (owners == own_index)[:, :, None] & (
        rank[:, :, None] == jnp.arange(capacity)[None, None, :]
    )
    send_slot = jnp.sum(
        jnp.where(chosen, block_slot.reshape(shards, per_dev)[:, :, None], 0), axis=1
    )
    picked = []
    for shift in range(1, shards):
        wanted = lax.dynamic_index_in_dim(
            send_slot, lax.rem(own_index + shift, shards), 0, keepdims=False
        )
        picked.append(pool_codes.at[wanted].get(mode="promise_in_bounds"))
    picked, question_hidden, recomp_hidden = lax.optimization_barrier(
        (picked, question_hidden, recomp_hidden)
    )
    got_codes = []
    for shift in range(1, shards):
        pairs = [(i, (i + shift) % shards) for i in range(shards)]
        got_codes.append(lax.ppermute(picked[shift - 1], "ctx", pairs))

    normed = jnp.concatenate(
        [rms_rows(question_hidden, norm_gain), rms_rows(recomp_hidden, norm_gain)], axis=0
    )
    pieces = lax.all_to_all(normed, "ctx", split_axis=1, concat_axis=0, tiled=True)
    arranged = pieces.reshape(shards, row_count, pieces.shape[1])
    question_part = arranged[:, :q_rows, :].reshape(shards * q_rows, pieces.shape[1])
    query = lax.psum_scatter(
        jnp.dot(question_part, w_query, preferred_element_type=jnp.float32),
        "ctx",
        scatter_dimension=0,
        tiled=True,
    ).astype(jnp.bfloat16)
    kv_weight = w_keyval.reshape(w_keyval.shape[0], 2 * kv_width)
    projected = lax.psum_scatter(
        jnp.dot(pieces, kv_weight, preferred_element_type=jnp.float32),
        "ctx",
        scatter_dimension=0,
        tiled=True,
    ).astype(jnp.bfloat16)
    own_kv = projected[:q_rows]
    extra = 16
    scale_count = pool_scales.size
    scale_rows = jnp.pad(
        pool_scales.reshape(1, -1), ((0, extra - 1), (0, 2 * kv_width - scale_count))
    )
    shared = lax.all_gather(
        jnp.concatenate([projected[q_rows:], scale_rows], axis=0), "ctx", axis=0, tiled=True
    )
    scales = (
        shared.reshape(shards, r_rows + extra, 2 * kv_width)[:, r_rows, :scale_count]
        .astype(jnp.float32)
        .reshape(-1)
    )
    where_to = jnp.pad(
        recomp_pos.reshape(shards, r_rows), ((0, 0), (0, extra)), constant_values=-1
    ).reshape(1, -1)
    every_query = lax.all_gather(query, "ctx", axis=0, tiled=True)

    sums, kv_cache = attend(
        owner,
        block_slot,
        scales,
        pool_codes,
        got_codes,
        every_query,
        shared,
        own_kv,
        where_to,
    )
    got = lax.all_to_all(
        sums.reshape(shards, q_rows, sums.shape[1]), "ctx", split_axis=0, concat_axis=0, tiled=True
    )
    terms = got[:, :, q_width:].astype(jnp.float32).reshape(shards, q_rows, 3, LANES)[..., :heads]
    got_lse = terms[:, :, 0] + terms[:, :, 1] + terms[:, :, 2]
    got_sums = got[:, :, :q_width]
    share = jnp.exp2(got_lse - jnp.max(got_lse, axis=0))
    share = share / jnp.sum(share, axis=0)
    attended = jnp.sum(
        got_sums.reshape(shards, q_rows, heads, HD).astype(jnp.float32) * share[..., None], axis=0
    )
    return (attended.reshape(q_rows, q_width).astype(jnp.bfloat16), kv_cache)


def solution(mesh):
    placed = (
        P(("groups", "ctx"), None),
        P(("groups", "ctx"), None),
        P(),
        P("ctx", "tp"),
        P("ctx", None, "tp"),
        P(("groups", "ctx"), None, None, "tp"),
        P(("groups", "ctx"), None, "tp"),
        P("groups", None),
        P("groups"),
        P("groups"),
    )
    return jax.shard_map(
        body,
        mesh=mesh,
        in_specs=placed,
        out_specs=(P(("groups", "ctx"), "tp"), P(None, ("groups", "ctx"), "tp")),
        check_vma=False,
    )
```
